1024 devices in a mesh: row: 8 (over x, core), col: 8 (over z_lo), grp: 16 (over y, z_hi).
Axes of the slice: x: 4, y: 4, z: 32 (z_hi: 4, z_lo: 8; z = z_hi * 8 + z_lo), core: 2. Of those that a mesh axis runs over, the one named last changes fastest.
Arguments:
- amplitudes: bfloat16 [512, 16, 1024], P(None, 'row', ('col', 'grp')), may hold values from -6 to 6
- ladder_integrals: bfloat16 [16, 1024, 64, 1024], P('row', None, 'grp', 'col'), may hold values from -0.046875 to 0.046875
- cycle_integrals: bfloat16 [16, 64, 16, 64], replicated, may hold values from -0.1875 to 0.1875
- pair_list: int32 [512, 2], replicated, may hold values from 0 to 127, as said below
- occ_energy: float32 [128], replicated, may hold values from -3 to -0.5
- batch_energy: float32 [64], replicated, may hold values from 0.2 to 4
- virt_energy: float32 [1024], P('col'), may hold values from 0.2 to 4
Outputs:
- update: float32 [16, 64, 32, 1024], P('row', None, 'grp', 'col')
The draws below stay inside these ranges and needn't reach their ends.
Inputs may be any that keep to these rules, and one draw needn't show every extreme that they name: `pair_list`: pair p holds the occupied orbital of window row p // 32 and that of window column p % 32; the 16 row orbitals and 32 column orbitals are all distinct.
All inputs are finite; a program needn't handle non-finite values.
Results may differ from the reference program's by a relative error of at most 0.0029.
Values may be sent and summed in bfloat16 or wider, within the bound.
A program may use at most 32 MiB of HBM per device.

```python
import jax
import jax.numpy as jnp
from jax import lax

NVIRT = 1024
NOCC = 128
OCC_I = 16
OCC_J = 32
NPAIR = 512
CBATCH = 16
ABATCH = 64


def draw_pair_list(key, part):
    order = jax.random.permutation(jax.random.fold_in(key, 7), NOCC).astype(jnp.int32)
    row_orbitals = order[:OCC_I]
    col_orbitals = order[OCC_I:OCC_I + OCC_J]
    first = jnp.broadcast_to(row_orbitals[:, None], (OCC_I, OCC_J))
    second = jnp.broadcast_to(col_orbitals[None, :], (OCC_I, OCC_J))
    return jnp.stack([first, second], axis=-1).reshape(OCC_I * OCC_J, 2).astype(jnp.int32)


def block_scale(own_key, dims, pieces, low, high):
    gain = 1.0
    for dim, blocks in pieces:
        draws = jax.random.uniform(jax.random.fold_in(jax.random.fold_in(own_key, 6), dim), (blocks,), jnp.float32, low / len(pieces), high / len(pieces))
        gain = gain * jnp.repeat(jnp.exp(draws), dims[dim] // blocks).reshape((-1,) + (1,) * (len(dims) - 1 - dim))
    return gain


def centred(stream_key, shape, spread, limit, cuts=(), dtype=jnp.bfloat16):
    result = spread * jax.random.normal(stream_key, shape, jnp.float32)
    if cuts:
        result = result * block_scale(stream_key, shape, cuts, -0.22, 0.18)
    return jnp.clip(result, -limit, limit).astype(dtype)


def setup_inputs(seed: int = 0) -> dict:
    seeds = jax.random.split(jax.random.key(seed), 8)
    amplitudes = centred(seeds[0], (NPAIR, CBATCH, NVIRT), 1.0, 6.0, ((1, 8), (2, 128)))
    ladder_integrals = centred(seeds[1], (CBATCH, NVIRT, ABATCH, NVIRT), (CBATCH * NVIRT) ** -0.5, 0.046875, ((0, 8), (2, 16), (3, 8)))
    cycle_integrals = centred(seeds[2], (OCC_I, ABATCH, OCC_I, ABATCH), (OCC_I * ABATCH) ** -0.5, 0.1875)
    pair_list = draw_pair_list(jax.random.fold_in(seeds[7], 71), 0)
    occ_energy = jnp.clip(jax.random.uniform(seeds[4], (NOCC,), jnp.float32, -3.0, -0.5), -3.0, -0.5)
    batch_energy = jnp.clip(jax.random.uniform(seeds[5], (ABATCH,), jnp.float32, 0.2, 4.0), 0.2, 4.0)
    virt_energy = jnp.clip(0.2 + 3.8 * jax.random.uniform(seeds[6], (NVIRT,), jnp.float32) ** block_scale(seeds[6], (NVIRT,), ((0, 8),), -0.2, 0.2), 0.2, 4.0)
    return {"amplitudes": amplitudes, "ladder_integrals": ladder_integrals, "cycle_integrals": cycle_integrals, "pair_list": pair_list, "occ_energy": occ_energy, "batch_energy": batch_energy, "virt_energy": virt_energy}


def reference(amplitudes, ladder_integrals, cycle_integrals, pair_list, occ_energy, batch_energy, virt_energy):
    def ladder_step(total, inputs):
        amp_slab, integral_slab = inputs
        flat = integral_slab.reshape(NVIRT, ABATCH * NVIRT)
        return total + jnp.dot(amp_slab, flat, preferred_element_type=jnp.float32), None

    start = jnp.zeros((NPAIR, ABATCH * NVIRT), jnp.float32)
    summed, unused = lax.scan(ladder_step, start, (jnp.transpose(amplitudes, (1, 0, 2)), ladder_integrals))
    ladder = summed.astype(jnp.bfloat16).reshape(OCC_I, OCC_J, ABATCH, NVIRT)
    regrouped = jnp.transpose(ladder, (0, 2, 1, 3))
    cycle = jnp.einsum("iakc,kcjb->iajb", cycle_integrals.astype(jnp.float32), regrouped.astype(jnp.float32))
    pair_grid = pair_list.reshape(OCC_I, OCC_J, 2)
    pair_energy = occ_energy[pair_grid[:, :, 0]] + occ_energy[pair_grid[:, :, 1]]
    denom = pair_energy[:, None, :, None] - batch_energy[None, :, None, None] - virt_energy[None, None, None, :]
    return (regrouped.astype(jnp.float32) + cycle) / denom
```

```python
import jax
import jax.numpy as jnp
from jax import lax
from jax.experimental import pallas as pl
from jax.experimental.pallas import tpu as pltpu
from jax.sharding import PartitionSpec as P

MESH = pl.DeviceIdType.MESH
F32 = jnp.float32
BF16 = jnp.bfloat16
NX, NY, NZ = 4, 4, 32
ROUNDS = 8


def dot(a, b, contract=((1,), (0,))):
    return lax.dot_general(a, b, (contract, ((), ())), preferred_element_type=F32)


def wrap(value, n):
    return lax.rem(value + 2 * n, n)


def kernel(
    amp_hbm, ladder_hbm, cycle_hbm, pair_ref, occ_ref, batch_ref, virt_ref, out_ref,
    buf, vraw, vwide, vmat, acc, sib, xsend, xrecv, ctmp, csend, crecv, dbuf,
    kraw, kwide, kmat, den,
    in_sem, zp_send, zp_recv, zm_send, zm_recv, yp_send, yp_recv, ym_send, ym_recv,
    hp_send, hp_recv, hm_send, hm_recv, s_send, s_recv, x_send, x_recv,
    c_send, c_recv, d_send, d_recv, e_send, e_recv,
):
    row = lax.axis_index("row")
    col = lax.axis_index("col")
    grp = lax.axis_index("grp")
    x, core = row // 2, lax.rem(row, 2)
    y = grp // 4
    z = lax.rem(grp, 4) * 8 + col

    def at(dx=0, dy=0, dz=0, flip=False):
        nx, ny, nz = wrap(x + dx, NX), wrap(y + dy, NY), wrap(z + dz, NZ)
        return (nx * 2 + (1 - core if flip else core), lax.rem(nz, 8), ny * 4 + nz // 8)

    def remote(src, dst, send, recv, device):
        return pltpu.make_async_remote_copy(
            src_ref=src, dst_ref=dst, send_sem=send, recv_sem=recv,
            device_id=device, device_id_type=MESH,
        )

    right, left = at(dz=1), at(dz=-1)
    up, down = at(dy=1), at(dy=-1)
    twin = at(flip=True)

    own_copy = pltpu.make_async_copy(amp_hbm, buf.at[0, 0], in_sem.at[0])
    v_copy = pltpu.make_async_copy(ladder_hbm, vraw, in_sem.at[1])
    k_copy = pltpu.make_async_copy(
        cycle_hbm.at[pl.ds(pl.multiple_of(row * 2048, 2048), 2048), :], kraw, in_sem.at[2]
    )
    own_copy.start()
    v_copy.start()
    k_copy.start()

    barrier = pltpu.get_barrier_semaphore()
    near = [right, left, up, down, twin, at(dx=1), at(dx=2), at(dx=3)]
    for device in near:
        pl.semaphore_signal(barrier, inc=1, device_id=device, device_id_type=MESH)
    pl.semaphore_wait(barrier, len(near))

    def z_plus(m, src):
        return remote(src, buf.at[0, 2 * m + 1], zp_send.at[m], zp_recv.at[m], right)

    def z_minus(m, src):
        return remote(src, buf.at[0, 2 * m + 2], zm_send.at[m], zm_recv.at[m], left)

    def four(slot, q):
        return buf.at[slot, pl.ds(4 * q, 4)]

    def y_plus(q):
        return remote(four(0, q), four(1, q), yp_send.at[q], yp_recv.at[q], up)

    def y_minus(q):
        return remote(four(0, q), four(2, q), ym_send.at[q], ym_recv.at[q], down)

    def half_plus(q):
        return remote(
            buf.at[1, pl.ds(4 * q, 2)], buf.at[3, pl.ds(4 * q, 2)],
            hp_send.at[q], hp_recv.at[q], up,
        )

    def half_minus(q):
        return remote(
            buf.at[2, pl.ds(4 * q + 2, 2)], buf.at[3, pl.ds(4 * q + 2, 2)],
            hm_send.at[q], hm_recv.at[q], down,
        )

    z_plus(0, amp_hbm).start()
    z_minus(0, amp_hbm).start()
    acc[...] = jnp.zeros_like(acc)
    own_copy.wait()
    v_copy.wait()

    def relayout(q):
        for slot, dy in enumerate((0, -1, 1, 2)):
            for e in range(4):
                dz = (2 * q, -2 * q - 1, 2 * q + 1, -2 * q - 2)[e]
                ny, nz = wrap(y + dy, NY), wrap(z + dz, NZ)
                shard = lax.rem(nz, 8) * 16 + ny * 4 + nz // 8
                for c in range(2):
                    start = pl.multiple_of(c * 4096 + shard * 32, 32)
                    to = ((slot * 4 + e) * 2 + c) * 32
                    vwide[pl.ds(to, 32), :] = vraw[pl.ds(start, 32), :].astype(F32)
        for a in range(4):
            vmat[q, :, pl.ds(a * 128, 128)] = vwide[pl.ds(a, 256, stride=4), :].astype(BF16)

    def multiply(q, block):
        lanes = pl.ds(pl.multiple_of(block * 128, 128), 128)
        lhs = buf[:, pl.ds(4 * q, 4), :, lanes].reshape(256, 128)
        product = dot(lhs, vmat[q], ((0,), (0,)))
        acc[0, block] += product[:, :256]
        acc[1, block] += product[:, 256:]

    @pl.loop(0, ROUNDS + 1)
    def _(q):
        @pl.when(q < ROUNDS)
        def _():
            for m in (2 * q, 2 * q + 1):
                z_plus(m, amp_hbm).wait_recv()

                @pl.when(m < 15)
                def _():
                    z_plus(m + 1, buf.at[0, 2 * m + 1]).start()
                    z_minus(m, amp_hbm).wait_recv()

                @pl.when(m < 14)
                def _():
                    z_minus(m + 1, buf.at[0, 2 * m + 2]).start()

            y_plus(q).start()
            y_minus(q).start()

        @pl.when(q > 0)
        def _():
            y_plus(q - 1).wait_recv()
            half_plus(q - 1).start()
            y_minus(q - 1).wait_recv()
            half_minus(q - 1).start()

        @pl.when(q < ROUNDS)
        def _():
            relayout(q)

        @pl.when(q > 1)
        def _():
            half_plus(q - 2).wait_recv()
            half_minus(q - 2).wait_recv()

            @pl.loop(0, 4)
            def _(block):
                multiply(q - 2, block)

    last = ROUNDS - 1
    half_plus(last).wait_recv()
    half_minus(last).wait_recv()

    def s_copy(dx):
        block = wrap(x + dx, NX)
        return remote(acc.at[1 - core, block], sib.at[block], s_send.at[dx], s_recv.at[dx], twin)

    def x_copy(dx):
        return remote(
            xsend.at[dx - 1], xrecv.at[dx - 1], x_send.at[dx - 1], x_recv.at[dx - 1], at(dx=dx)
        )

    for dx in (2, 1, 3, 0):
        multiply(last, wrap(x + dx, NX))
        s_copy(dx).start()
    for dx in (2, 1, 3):
        block = wrap(x + dx, NX)
        s_copy(dx).wait_recv()
        xsend[dx - 1] = acc[core, block] + sib[block]
        x_copy(dx).start()

    k_copy.wait()
    kwide[...] = kraw[...].astype(F32)
    from_c = lax.broadcasted_iota(jnp.int32, (64, 256), 0)
    lane = lax.broadcasted_iota(jnp.int32, (64, 256), 1)
    lane_c = (lane % 128) // 8 * 4 + lane // 128 * 2 + lane % 2
    places = [
        jnp.where((lane_c == from_c) & (lane % 8 // 2 == i), 1.0, 0.0).astype(BF16)
        for i in range(4)
    ]
    for nx in range(4):
        total = jnp.zeros((128, 256), F32)
        for i in range(4):
            part = kwide[pl.ds(nx * 4 + i, 128, stride=16), :].astype(BF16)
            total = total + dot(part, places[i])
        kmat[nx * 2] = total[:, :128].astype(BF16)
        kmat[nx * 2 + 1] = total[:, 128:].astype(BF16)

    s_copy(0).wait_recv()
    ladder = acc[core, x] + sib[x]
    for dx in (1, 3, 2):
        x_copy(dx).wait_recv()
        ladder = ladder + xrecv[dx - 1]

    for i in range(4):
        for a in range(2):
            ctmp[pl.ds(i * 2 + a, 32, stride=8), :] = ladder[
                i * 32:(i + 1) * 32, a * 128:(a + 1) * 128
            ]
    csend[...] = ctmp[...].astype(BF16).reshape(16, 16, 128)

    def c_copy(d):
        other = lax.rem(grp + d, 16)
        return remote(
            csend.at[other], crecv.at[grp], c_send.at[d], c_recv.at[d], (row, col, other)
        )

    order = (2, 6, 10, 14, 1, 3, 5, 7, 9, 11, 13, 15, 4, 8, 12)
    for d in order:
        c_copy(d).start()
    crecv[grp] = csend[grp]

    def column(ref, n):
        wide = jnp.broadcast_to(ref[...], (n, n))
        diagonal = lax.broadcasted_iota(jnp.int32, (n, n), 0) == lax.broadcasted_iota(
            jnp.int32, (n, n), 1
        )
        return jnp.sum(jnp.where(diagonal, wide, 0.0), axis=1, keepdims=True)

    occ = column(occ_ref, 128)
    orbital = lax.broadcasted_iota(jnp.int32, (128, 512), 0)
    first = jnp.sum(jnp.where(pair_ref[0:1, :] == orbital, occ, 0.0), axis=0, keepdims=True)
    second = jnp.sum(jnp.where(pair_ref[1:2, :] == orbital, occ, 0.0), axis=0, keepdims=True)
    energy = first + second
    pair = lax.broadcasted_iota(jnp.int32, (1, 512), 1)
    batch = column(batch_ref, 64)
    for i in range(2):
        for j in range(2):
            mine = (row * 2 + i) * 32 + grp * 2 + j
            one = jnp.sum(jnp.where(pair == mine, energy, 0.0), axis=1, keepdims=True)
            den[i, j] = one - batch - virt_ref[...]

    for d in order:
        c_copy(d).wait_recv()
    blocks = crecv[...].astype(F32).reshape(16, 2, 8, 128)
    for j in range(2):
        dbuf[x, core, :, pl.ds(j * 128, 128)] = blocks[:, j].reshape(128, 128).astype(BF16)

    def d_copy(dx):
        return remote(
            dbuf.at[x, core], dbuf.at[x, core], d_send.at[dx - 1], d_recv.at[dx - 1], at(dx=dx)
        )

    def e_copy(dx):
        block = dbuf.at[wrap(x - dx, NX), core]
        return remote(block, block, e_send.at[dx], e_recv.at[dx], twin)

    for dx in (2, 1, 3):
        d_copy(dx).start()
    e_copy(0).start()

    out_row = lax.broadcasted_iota(jnp.int32, (128, 128), 0)
    lane = lax.broadcasted_iota(jnp.int32, (128, 128), 1)
    same = (out_row % 64 // 4 == lane // 8) & (out_row % 2 == lane % 2)
    same = same & (core * 2 + out_row // 64 == lane % 8 // 2)

    def pick(part):
        return jnp.where(same & (out_row % 4 // 2 == part), 1.0, 0.0).astype(BF16)

    def term(dx, part):
        block = wrap(x - dx, NX)
        return dot(kmat[block * 2 + part], dbuf[block, part])

    total = term(0, core) + dot(pick(core), dbuf[x, core])
    for dx in (1, 3, 2):
        d_copy(dx).wait_recv()
        e_copy(dx).start()
        total = total + term(dx, core)
    e_copy(0).wait_recv()
    total = total + term(0, 1 - core) + dot(pick(1 - core), dbuf[x, 1 - core])
    for dx in (1, 3, 2):
        e_copy(dx).wait_recv()
        total = total + term(dx, 1 - core)
    for i in range(2):
        for j in range(2):
            value = total[i * 64:(i + 1) * 64, j * 128:(j + 1) * 128] / den[i, j]
            out_ref[pl.ds(i * 128 + j, 64, stride=2), :] = value

    @pl.loop(0, 16)
    def _(m):
        z_plus(m, buf.at[0, 0]).wait_send()

        @pl.when(m < 15)
        def _():
            z_minus(m, buf.at[0, 0]).wait_send()

    @pl.loop(0, ROUNDS)
    def _(q):
        y_plus(q).wait_send()
        y_minus(q).wait_send()
        half_plus(q).wait_send()
        half_minus(q).wait_send()

    for dx in range(4):
        s_copy(dx).wait_send()
        e_copy(dx).wait_send()
        if dx:
            x_copy(dx).wait_send()
            d_copy(dx).wait_send()
    for d in order:
        c_copy(d).wait_send()


def local(
    amplitudes, ladder_integrals, cycle_integrals, pair_list, occ_energy, batch_energy, virt_energy
):
    any_spec = pl.BlockSpec(memory_space=pl.ANY)
    vmem = pl.BlockSpec(memory_space=pltpu.VMEM)
    dma = pltpu.SemaphoreType.DMA
    counts = (3, 16, 16, 15, 15, 8, 8, 8, 8, 8, 8, 8, 8, 4, 4, 3, 3, 16, 16, 3, 3, 4, 4)
    out = pl.pallas_call(
        kernel,
        out_shape=jax.ShapeDtypeStruct((256, 128), F32),
        in_specs=[any_spec] * 3 + [vmem] * 4,
        out_specs=vmem,
        scratch_shapes=[
            pltpu.VMEM((4, 32, 16, 512), BF16),
            pltpu.VMEM((8192, 128), BF16),
            pltpu.VMEM((1024, 128), F32),
            pltpu.VMEM((8, 256, 512), BF16),
            pltpu.VMEM((2, 4, 128, 256), F32),
            pltpu.VMEM((4, 128, 256), F32),
            pltpu.VMEM((3, 128, 256), F32),
            pltpu.VMEM((3, 128, 256), F32),
            pltpu.VMEM((256, 128), F32),
            pltpu.VMEM((16, 16, 128), BF16),
            pltpu.VMEM((16, 16, 128), BF16),
            pltpu.VMEM((4, 2, 128, 256), BF16),
            pltpu.VMEM((2048, 64), BF16),
            pltpu.VMEM((2048, 64), F32),
            pltpu.VMEM((8, 128, 128), BF16),
            pltpu.VMEM((2, 2, 64, 128), F32),
        ] + [dma((n,)) for n in counts],
        compiler_params=pltpu.CompilerParams(
            collective_id=0, has_side_effects=True, vmem_limit_bytes=48 * 1024 * 1024
        ),
    )(
        jnp.transpose(amplitudes, (1, 2, 0)).reshape(16, 512),
        ladder_integrals.reshape(8192, 128),
        cycle_integrals.reshape(16384, 64),
        jnp.transpose(pair_list),
        occ_energy.reshape(1, 128),
        batch_energy.reshape(1, 64),
        virt_energy.reshape(1, 128),
    )
    return out.reshape(2, 64, 2, 128)


def solution(mesh):
    placed = (
        P(None, "row", ("col", "grp")),
        P("row", None, "grp", "col"),
        P(),
        P(),
        P(),
        P(),
        P("col"),
    )
    return jax.shard_map(
        local, mesh=mesh, in_specs=placed, out_specs=P("row", None, "grp", "col"), check_vma=False
    )
```

```python
import jax
import jax.numpy as jnp
from jax import lax
from jax.experimental import pallas as pl
from jax.experimental.pallas import tpu as pltpu
from jax.sharding import PartitionSpec as P

MESH = pl.DeviceIdType.MESH
F32 = jnp.float32
BF16 = jnp.bfloat16
NX, NY, NZ = 4, 4, 32
ROUNDS = 8


def dot(a, b, contract=((1,), (0,))):
    return lax.dot_general(a, b, (contract, ((), ())), preferred_element_type=F32)


def wrap(value, n):
    return lax.rem(value + 2 * n, n)


def kernel(
    amp_hbm, ladder_hbm, cycle_hbm, pair_hbm, occ_hbm, batch_hbm, virt_hbm, out_ref,
    pair_ref, occ_ref, batch_ref, virt_ref, buf, vraw, vwide, vmat, acc, sib, xsend, xrecv, ctmp, csend, crecv, dbuf,
    kraw, kwide, kmat, den,
    in_sem, z_send, z_recv, yp_send, yp_recv, ym_send, ym_recv,
    hp_send, hp_recv, hm_send, hm_recv, s_send, s_recv, x_send, x_recv,
    c_send, c_recv, d_send, d_recv, e_send, e_recv,
):
    row = lax.axis_index("row")
    col = lax.axis_index("col")
    grp = lax.axis_index("grp")
    x, core = row // 2, lax.rem(row, 2)
    y = grp // 4
    z = lax.rem(grp, 4) * 8 + col

    def at(dx=0, dy=0, dz=0, flip=False):
        nx, ny, nz = wrap(x + dx, NX), wrap(y + dy, NY), wrap(z + dz, NZ)
        return (nx * 2 + (1 - core if flip else core), lax.rem(nz, 8), ny * 4 + nz // 8)

    def remote(src, dst, send, recv, device):
        return pltpu.make_async_remote_copy(
            src_ref=src, dst_ref=dst, send_sem=send, recv_sem=recv,
            device_id=device, device_id_type=MESH,
        )

    up, down = at(dy=1), at(dy=-1)
    twin = at(flip=True)

    own_copy = pltpu.make_async_copy(amp_hbm, buf.at[0, 0], in_sem.at[0])
    v_copy = pltpu.make_async_copy(ladder_hbm, vraw, in_sem.at[1])
    k_copy = pltpu.make_async_copy(
        cycle_hbm.at[pl.ds(pl.multiple_of(row * 2048, 2048), 2048), :], kraw, in_sem.at[2]
    )
    small = [
        pltpu.make_async_copy(src, dst, in_sem.at[3 + i])
        for i, (src, dst) in enumerate(
            ((pair_hbm, pair_ref), (occ_hbm, occ_ref), (batch_hbm, batch_ref), (virt_hbm, virt_ref))
        )
    ]
    own_copy.start()
    v_copy.start()
    k_copy.start()
    for copy in small:
        copy.start()

    barrier = pltpu.get_barrier_semaphore()
    near = [at(dz=d) for d in (1, -1, 2, -2, 3, -3, 4, -4)]
    near += [up, down, twin, at(dx=1), at(dx=2), at(dx=3)]
    for device in near:
        pl.semaphore_signal(barrier, inc=1, device_id=device, device_id_type=MESH)
    pl.semaphore_wait(barrier, len(near))

    def place(t):
        return 2 * t - 1 if t > 0 else -2 * t

    def z_copy(t):
        sign, far = (1, t) if t > 0 else (-1, -t)
        step = far % 4 or 4
        source = amp_hbm if far == step else buf.at[0, place(sign * (far - step))]
        return remote(
            source, buf.at[0, place(t)], z_send.at[place(t)], z_recv.at[place(t)], at(dz=sign * step)
        )

    def pass_on(*heads):
        for more in (4, 1, 2, 3):
            for sign, far in heads:
                if sign * (far + more) != -16:
                    z_copy(sign * (far + more)).start()

    def arrived(*shards):
        for t in shards:
            z_copy(t).wait_recv()

    def four(slot, q):
        return buf.at[slot, pl.ds(4 * q, 4)]

    def y_plus(q):
        return remote(four(0, q), four(1, q), yp_send.at[q], yp_recv.at[q], up)

    def y_minus(q):
        return remote(four(0, q), four(2, q), ym_send.at[q], ym_recv.at[q], down)

    def half_plus(q):
        return remote(
            buf.at[1, pl.ds(4 * q, 2)], buf.at[3, pl.ds(4 * q, 2)],
            hp_send.at[q], hp_recv.at[q], up,
        )

    def half_minus(q):
        return remote(
            buf.at[2, pl.ds(4 * q + 2, 2)], buf.at[3, pl.ds(4 * q + 2, 2)],
            hm_send.at[q], hm_recv.at[q], down,
        )

    pass_on((1, 0), (-1, 0))
    acc[...] = jnp.zeros_like(acc)
    own_copy.wait()
    v_copy.wait()

    def relayout(q):
        for slot, dy in enumerate((0, -1, 1, 2)):
            for e in range(4):
                dz = (2 * q, -2 * q - 1, 2 * q + 1, -2 * q - 2)[e]
                ny, nz = wrap(y + dy, NY), wrap(z + dz, NZ)
                shard = lax.rem(nz, 8) * 16 + ny * 4 + nz // 8
                for c in range(2):
                    start = pl.multiple_of(c * 4096 + shard * 32, 32)
                    to = ((slot * 4 + e) * 2 + c) * 32
                    vwide[pl.ds(to, 32), :] = vraw[pl.ds(start, 32), :].astype(F32)
        for a in range(4):
            vmat[q, :, pl.ds(a * 128, 128)] = vwide[pl.ds(a, 256, stride=4), :].astype(BF16)

    def multiply(q, block):
        lanes = pl.ds(pl.multiple_of(block * 128, 128), 128)
        lhs = buf[:, pl.ds(4 * q, 4), :, lanes].reshape(256, 128)
        product = dot(lhs, vmat[q], ((0,), (0,)))
        acc[0, block] += product[:, :256]
        acc[1, block] += product[:, 256:]

    @pl.loop(0, ROUNDS)
    def _(q):
        relayout(q)

    def y_start(q):
        y_plus(q).start()
        y_minus(q).start()

    def y_next(q):
        y_plus(q).wait_recv()
        half_plus(q).start()
        y_minus(q).wait_recv()
        half_minus(q).start()

    def y_done(q):
        half_plus(q).wait_recv()
        half_minus(q).wait_recv()

    def products(q):
        y_done(q)

        @pl.loop(0, 4)
        def _(block):
            multiply(q, block)

    last = ROUNDS - 1
    arrived(1, -1, 2)
    y_start(0)
    arrived(-2, 3, -3, 4, -4)
    pass_on((1, 4), (-1, 4))
    y_start(1)
    y_next(0)
    arrived(5, -5, 6)
    y_start(2)
    y_next(1)
    arrived(-6, 7, -7, 8, -8)
    pass_on((1, 8), (-1, 8))
    y_start(3)
    products(0)
    y_next(2)
    products(1)
    arrived(9, -9, 10)
    y_start(4)
    y_next(3)
    arrived(-10, 11, -11, 12, -12)
    pass_on((1, 12), (-1, 12))
    y_start(5)
    products(2)
    products(3)
    y_next(4)
    arrived(13, -13, 14)
    y_start(6)
    y_next(5)
    arrived(-14, 15, -15, 16)
    y_start(7)
    products(4)
    products(5)
    y_next(6)
    y_next(7)
    products(6)
    y_done(last)

    def s_copy(dx):
        block = wrap(x + dx, NX)
        return remote(acc.at[1 - core, block], sib.at[block], s_send.at[dx], s_recv.at[dx], twin)

    def x_copy(dx):
        return remote(
            xsend.at[dx - 1], xrecv.at[dx - 1], x_send.at[dx - 1], x_recv.at[dx - 1], at(dx=dx)
        )

    for dx in (2, 1, 3, 0):
        multiply(last, wrap(x + dx, NX))
        s_copy(dx).start()
    for dx in (2, 1, 3):
        block = wrap(x + dx, NX)
        s_copy(dx).wait_recv()
        xsend[dx - 1] = acc[core, block] + sib[block]
        x_copy(dx).start()

    k_copy.wait()
    kwide[...] = kraw[...].astype(F32)
    from_c = lax.broadcasted_iota(jnp.int32, (64, 256), 0)
    lane = lax.broadcasted_iota(jnp.int32, (64, 256), 1)
    lane_c = (lane % 128) // 8 * 4 + lane // 128 * 2 + lane % 2
    places = [
        jnp.where((lane_c == from_c) & (lane % 8 // 2 == i), 1.0, 0.0).astype(BF16)
        for i in range(4)
    ]
    for nx in range(4):
        total = jnp.zeros((128, 256), F32)
        for i in range(4):
            part = kwide[pl.ds(nx * 4 + i, 128, stride=16), :].astype(BF16)
            total = total + dot(part, places[i])
        kmat[nx * 2] = total[:, :128].astype(BF16)
        kmat[nx * 2 + 1] = total[:, 128:].astype(BF16)

    s_copy(0).wait_recv()
    ladder = acc[core, x] + sib[x]
    for dx in (1, 3, 2):
        x_copy(dx).wait_recv()
        ladder = ladder + xrecv[dx - 1]

    for i in range(4):
        for a in range(2):
            ctmp[pl.ds(i * 2 + a, 32, stride=8), :] = ladder[
                i * 32:(i + 1) * 32, a * 128:(a + 1) * 128
            ]
    csend[...] = ctmp[...].astype(BF16).reshape(16, 16, 128)

    def c_copy(d):
        other = lax.rem(grp + d, 16)
        return remote(
            csend.at[other], crecv.at[grp], c_send.at[d], c_recv.at[d], (row, col, other)
        )

    order = (2, 6, 10, 14, 1, 3, 5, 7, 9, 11, 13, 15, 4, 8, 12)
    for d in order:
        c_copy(d).start()
    crecv[grp] = csend[grp]

    for copy in small:
        copy.wait()
    def column(ref, n):
        wide = jnp.broadcast_to(ref[...], (n, n))
        diagonal = lax.broadcasted_iota(jnp.int32, (n, n), 0) == lax.broadcasted_iota(
            jnp.int32, (n, n), 1
        )
        return jnp.sum(jnp.where(diagonal, wide, 0.0), axis=1, keepdims=True)

    occ = column(occ_ref, 128)
    orbital = lax.broadcasted_iota(jnp.int32, (128, 512), 0)
    first = jnp.sum(jnp.where(pair_ref[0:1, :] == orbital, occ, 0.0), axis=0, keepdims=True)
    second = jnp.sum(jnp.where(pair_ref[1:2, :] == orbital, occ, 0.0), axis=0, keepdims=True)
    energy = first + second
    pair = lax.broadcasted_iota(jnp.int32, (1, 512), 1)
    batch = column(batch_ref, 64)
    for i in range(2):
        for j in range(2):
            mine = (row * 2 + i) * 32 + grp * 2 + j
            one = jnp.sum(jnp.where(pair == mine, energy, 0.0), axis=1, keepdims=True)
            den[i, j] = one - batch - virt_ref[...]

    for d in order:
        c_copy(d).wait_recv()
    blocks = crecv[...].astype(F32).reshape(16, 2, 8, 128)
    for j in range(2):
        dbuf[x, core, :, pl.ds(j * 128, 128)] = blocks[:, j].reshape(128, 128).astype(BF16)

    def d_copy(dx):
        return remote(
            dbuf.at[x, core], dbuf.at[x, core], d_send.at[dx - 1], d_recv.at[dx - 1], at(dx=dx)
        )

    def e_copy(dx):
        block = dbuf.at[wrap(x - dx, NX), core]
        return remote(block, block, e_send.at[dx], e_recv.at[dx], twin)

    for dx in (2, 1, 3):
        d_copy(dx).start()
    e_copy(0).start()

    out_row = lax.broadcasted_iota(jnp.int32, (128, 128), 0)
    lane = lax.broadcasted_iota(jnp.int32, (128, 128), 1)
    same = (out_row % 64 // 4 == lane // 8) & (out_row % 2 == lane % 2)
    same = same & (core * 2 + out_row // 64 == lane % 8 // 2)

    def pick(part):
        return jnp.where(same & (out_row % 4 // 2 == part), 1.0, 0.0).astype(BF16)

    def term(dx, part):
        block = wrap(x - dx, NX)
        return dot(kmat[block * 2 + part], dbuf[block, part])

    total = term(0, core) + dot(pick(core), dbuf[x, core])
    for dx in (1, 3, 2):
        d_copy(dx).wait_recv()
        e_copy(dx).start()
        total = total + term(dx, core)
    e_copy(0).wait_recv()
    total = total + term(0, 1 - core) + dot(pick(1 - core), dbuf[x, 1 - core])
    for dx in (1, 3, 2):
        e_copy(dx).wait_recv()
        total = total + term(dx, 1 - core)
    for i in range(2):
        for j in range(2):
            value = total[i * 64:(i + 1) * 64, j * 128:(j + 1) * 128] / den[i, j]
            out_ref[pl.ds(i * 128 + j, 64, stride=2), :] = value

    for t in range(-15, 17):
        if t:
            z_copy(t).wait_send()

    @pl.loop(0, ROUNDS)
    def _(q):
        y_plus(q).wait_send()
        y_minus(q).wait_send()
        half_plus(q).wait_send()
        half_minus(q).wait_send()

    for dx in range(4):
        s_copy(dx).wait_send()
        e_copy(dx).wait_send()
        if dx:
            x_copy(dx).wait_send()
            d_copy(dx).wait_send()
    for d in order:
        c_copy(d).wait_send()


def local(
    amplitudes, ladder_integrals, cycle_integrals, pair_list, occ_energy, batch_energy, virt_energy
):
    hbm = pl.BlockSpec(memory_space=pltpu.HBM)
    dma = pltpu.SemaphoreType.DMA
    counts = (7, 32, 32, 8, 8, 8, 8, 8, 8, 8, 8, 4, 4, 3, 3, 16, 16, 3, 3, 4, 4)
    out = pl.pallas_call(
        kernel,
        out_shape=jax.ShapeDtypeStruct((256, 128), F32),
        in_specs=[hbm] * 7,
        out_specs=pl.BlockSpec(memory_space=pltpu.VMEM),
        scratch_shapes=[
            pltpu.VMEM((2, 512), jnp.int32),
            pltpu.VMEM((1, 128), F32),
            pltpu.VMEM((1, 64), F32),
            pltpu.VMEM((1, 128), F32),
            pltpu.VMEM((4, 32, 16, 512), BF16),
            pltpu.VMEM((8192, 128), BF16),
            pltpu.VMEM((1024, 128), F32),
            pltpu.VMEM((8, 256, 512), BF16),
            pltpu.VMEM((2, 4, 128, 256), F32),
            pltpu.VMEM((4, 128, 256), F32),
            pltpu.VMEM((3, 128, 256), F32),
            pltpu.VMEM((3, 128, 256), F32),
            pltpu.VMEM((256, 128), F32),
            pltpu.VMEM((16, 16, 128), BF16),
            pltpu.VMEM((16, 16, 128), BF16),
            pltpu.VMEM((4, 2, 128, 256), BF16),
            pltpu.VMEM((2048, 64), BF16),
            pltpu.VMEM((2048, 64), F32),
            pltpu.VMEM((8, 128, 128), BF16),
            pltpu.VMEM((2, 2, 64, 128), F32),
        ] + [dma((n,)) for n in counts],
        compiler_params=pltpu.CompilerParams(
            collective_id=0, has_side_effects=True, vmem_limit_bytes=48 * 1024 * 1024
        ),
    )(
        jnp.transpose(amplitudes, (1, 2, 0)).reshape(16, 512),
        ladder_integrals.reshape(8192, 128),
        cycle_integrals.reshape(16384, 64),
        jnp.transpose(pair_list),
        occ_energy.reshape(1, 128),
        batch_energy.reshape(1, 64),
        virt_energy.reshape(1, 128),
    )
    return out.reshape(2, 64, 2, 128)


def solution(mesh):
    placed = (
        P(None, "row", ("col", "grp")),
        P("row", None, "grp", "col"),
        P(),
        P(),
        P(),
        P(),
        P("col"),
    )
    return jax.shard_map(
        local, mesh=mesh, in_specs=placed, out_specs=P("row", None, "grp", "col"), check_vma=False
    )
```

```python
import jax
import jax.numpy as jnp
from jax import lax
from jax.experimental import pallas as pl
from jax.experimental.pallas import tpu as pltpu
from jax.sharding import PartitionSpec as P

MESH = pl.DeviceIdType.MESH
F32 = jnp.float32
BF16 = jnp.bfloat16
NX, NY, NZ = 4, 4, 32
ROUNDS = 8
DIRECT = 6


def dot(a, b, contract=((1,), (0,))):
    return lax.dot_general(a, b, (contract, ((), ())), preferred_element_type=F32)


def wrap(value, n):
    return lax.rem(value + 2 * n, n)


def kernel(
    amp_hbm, ladder_hbm, cycle_hbm, pair_hbm, occ_hbm, batch_hbm, virt_hbm, out_ref,
    pair_ref, occ_ref, batch_ref, virt_ref, buf, vraw, vwide, vmat, acc, sib, xsend, xrecv, xfar, ctmp, csend, crecv, dnear, dfar,
    kraw, kwide, kmat, kfar, den,
    in_sem, z_send, z_recv, yp_send, yp_recv, ym_send, ym_recv,
    hp_send, hp_recv, hm_send, hm_recv, s_send, s_recv, x_send, x_recv,
    c_send, c_recv, d_send, d_recv, e_send, e_recv,
):
    row = lax.axis_index("row")
    col = lax.axis_index("col")
    grp = lax.axis_index("grp")
    x, core = row // 2, lax.rem(row, 2)
    y = grp // 4
    z = lax.rem(grp, 4) * 8 + col

    def at(dx=0, dy=0, dz=0, flip=False):
        nx, ny, nz = wrap(x + dx, NX), wrap(y + dy, NY), wrap(z + dz, NZ)
        return (nx * 2 + (1 - core if flip else core), lax.rem(nz, 8), ny * 4 + nz // 8)

    def remote(src, dst, send, recv, device):
        return pltpu.make_async_remote_copy(
            src_ref=src, dst_ref=dst, send_sem=send, recv_sem=recv,
            device_id=device, device_id_type=MESH,
        )

    up, down = at(dy=1), at(dy=-1)
    twin = at(flip=True)

    own_copy = pltpu.make_async_copy(amp_hbm, buf.at[0, 0], in_sem.at[0])
    v_copy = pltpu.make_async_copy(ladder_hbm, vraw, in_sem.at[1])
    k_copy = pltpu.make_async_copy(
        cycle_hbm.at[pl.ds(pl.multiple_of(row * 2048, 2048), 2048), :], kraw, in_sem.at[2]
    )
    small = [
        pltpu.make_async_copy(src, dst, in_sem.at[3 + i])
        for i, (src, dst) in enumerate(
            ((pair_hbm, pair_ref), (occ_hbm, occ_ref), (batch_hbm, batch_ref), (virt_hbm, virt_ref))
        )
    ]
    own_copy.start()
    v_copy.start()
    k_copy.start()
    for copy in small:
        copy.start()

    barrier = pltpu.get_barrier_semaphore()
    near = [at(dz=d) for d in (1, -1, 2, -2, 3, -3, 4, -4)]
    near += [at(dy=2), up, down, twin, at(dx=1), at(dx=2), at(dx=3)]
    for device in near:
        pl.semaphore_signal(barrier, inc=1, device_id=device, device_id_type=MESH)
    pl.semaphore_wait(barrier, len(near))

    def place(t):
        return 2 * t - 1 if t > 0 else -2 * t

    def z_copy(t):
        sign, far = (1, t) if t > 0 else (-1, -t)
        step = far % 4 or 4
        source = amp_hbm if far == step else buf.at[0, place(sign * (far - step))]
        return remote(
            source, buf.at[0, place(t)], z_send.at[place(t)], z_recv.at[place(t)], at(dz=sign * step)
        )

    def pass_on(*heads):
        for more in (4, 1, 2, 3):
            for sign, far in heads:
                if sign * (far + more) != -16:
                    z_copy(sign * (far + more)).start()

    def arrived(*shards):
        for t in shards:
            z_copy(t).wait_recv()

    def four(slot, q):
        return buf.at[slot, pl.ds(4 * q, 4)]

    def y_plus(q):
        return remote(four(0, q), four(1, q), yp_send.at[q], yp_recv.at[q], up)

    def y_minus(q):
        return remote(four(0, q), four(2, q), ym_send.at[q], ym_recv.at[q], down)

    def half_plus(q):
        return remote(
            buf.at[1, pl.ds(4 * q, 2)], buf.at[3, pl.ds(4 * q, 2)],
            hp_send.at[q], hp_recv.at[q], up,
        )

    def half_minus(q):
        return remote(
            buf.at[2, pl.ds(4 * q + 2, 2)], buf.at[3, pl.ds(4 * q + 2, 2)],
            hm_send.at[q], hm_recv.at[q], down,
        )

    def y_two(q):
        return remote(four(0, q), four(3, q), hp_send.at[q], hp_recv.at[q], at(dy=2))

    pass_on((1, 0), (-1, 0))
    acc[...] = jnp.zeros_like(acc)
    own_copy.wait()
    v_copy.wait()

    def relayout(q):
        for slot, dy in enumerate((0, -1, 1, 2)):
            for e in range(4):
                dz = (2 * q, -2 * q - 1, 2 * q + 1, -2 * q - 2)[e]
                ny, nz = wrap(y + dy, NY), wrap(z + dz, NZ)
                shard = lax.rem(nz, 8) * 16 + ny * 4 + nz // 8
                for c in range(2):
                    start = pl.multiple_of(c * 4096 + shard * 32, 32)
                    to = ((slot * 4 + e) * 2 + c) * 32
                    vwide[pl.ds(to, 32), :] = vraw[pl.ds(start, 32), :].astype(F32)
        for a in range(4):
            vmat[q, :, pl.ds(a * 128, 128)] = vwide[pl.ds(a, 256, stride=4), :].astype(BF16)

    def multiply(q, block):
        lanes = pl.ds(pl.multiple_of(block * 128, 128), 128)
        lhs = buf[:, pl.ds(4 * q, 4), :, lanes].reshape(256, 128)
        product = dot(lhs, vmat[q], ((0,), (0,)))
        acc[0, block] += product[:, :256]
        acc[1, block] += product[:, 256:]

    @pl.loop(0, ROUNDS)
    def _(q):
        relayout(q)

    def y_start(q):
        if q >= DIRECT:
            y_two(q).start()
        y_plus(q).start()
        y_minus(q).start()

    def y_next(q):
        y_plus(q).wait_recv()
        if q < DIRECT:
            half_plus(q).start()
        y_minus(q).wait_recv()
        if q < DIRECT:
            half_minus(q).start()

    def y_done(q):
        if q >= DIRECT:
            y_two(q).wait_recv()
            return
        half_plus(q).wait_recv()
        half_minus(q).wait_recv()

    def products(q):
        y_done(q)

        @pl.loop(0, 4)
        def _(block):
            multiply(q, block)

    last = ROUNDS - 1
    arrived(1, -1, 2)
    y_start(0)
    arrived(-2, 3, -3, 4, -4)
    pass_on((1, 4), (-1, 4))
    y_start(1)
    y_next(0)
    arrived(5, -5, 6)
    y_start(2)
    y_next(1)
    arrived(-6, 7, -7, 8, -8)
    pass_on((1, 8), (-1, 8))
    y_start(3)
    products(0)
    y_next(2)
    products(1)
    arrived(9, -9, 10)
    y_start(4)
    y_next(3)
    arrived(-10, 11, -11, 12, -12)
    pass_on((1, 12), (-1, 12))
    y_start(5)
    products(2)
    products(3)
    y_next(4)
    arrived(13, -13, 14)
    y_start(6)
    y_next(5)
    arrived(-14, 15, -15, 16)
    y_start(7)
    products(4)
    products(5)
    y_next(6)
    y_next(7)
    products(6)
    y_done(last)

    def s_copy(dx):
        block = wrap(x + dx, NX)
        return remote(acc.at[1 - core, block], sib.at[block], s_send.at[dx], s_recv.at[dx], twin)

    def x_copy(dx):
        src, dst = (xfar.at[0], xfar.at[1]) if dx == 2 else (xsend.at[dx // 2], xrecv.at[dx // 2])
        return remote(src, dst, x_send.at[dx - 1], x_recv.at[dx - 1], at(dx=dx))

    for dx in (2, 1, 3, 0):
        multiply(last, wrap(x + dx, NX))
        s_copy(dx).start()
    for dx in (2, 1, 3):
        block = wrap(x + dx, NX)
        s_copy(dx).wait_recv()
        both = acc[core, block] + sib[block]
        if dx == 2:
            xfar[0] = both.astype(BF16)
        else:
            xsend[dx // 2] = both
        x_copy(dx).start()

    k_copy.wait()
    kwide[...] = kraw[...].astype(F32)
    from_c = lax.broadcasted_iota(jnp.int32, (64, 256), 0)
    lane = lax.broadcasted_iota(jnp.int32, (64, 256), 1)
    y_part = lane % 32 // 8 * 16 + lane % 2
    step_part = lane % 128 // 32
    from_zh = lax.rem(grp + jnp.where(step_part == 2, 3, step_part), 4)
    near_c = y_part + from_zh * 4 + lane // 128 * 2
    far_c = y_part + lax.rem(grp + 2, 4) * 4 + lane // 32 % 2 * 2
    far_total = jnp.zeros((128, 256), F32)
    for nx in range(4):
        total = jnp.zeros((128, 256), F32)
        for i in range(4):
            part = kwide[pl.ds(nx * 4 + i, 128, stride=16), :].astype(BF16)
            mine = lane % 8 // 2 == i
            total = total + dot(part, jnp.where(mine & (near_c == from_c), 1.0, 0.0).astype(BF16))
            mine = mine & (lane // 64 == nx) & (far_c == from_c)
            far_total = far_total + dot(part, jnp.where(mine, 1.0, 0.0).astype(BF16))
        kmat[nx * 2] = total[:, :128].astype(BF16)
        kmat[nx * 2 + 1] = total[:, 128:].astype(BF16)
    kfar[...] = far_total.astype(BF16)

    s_copy(0).wait_recv()
    ladder = acc[core, x] + sib[x]
    for dx in (1, 3, 2):
        x_copy(dx).wait_recv()
        ladder = ladder + (xfar[1].astype(F32) if dx == 2 else xrecv[dx // 2])

    for i in range(4):
        for a in range(2):
            ctmp[pl.ds(i * 2 + a, 32, stride=8), :] = ladder[
                i * 32:(i + 1) * 32, a * 128:(a + 1) * 128
            ]
    csend[...] = ctmp[...].astype(BF16).reshape(16, 16, 128)

    def c_copy(d):
        other = lax.rem(grp + d, 16)
        return remote(
            csend.at[other], crecv.at[grp], c_send.at[d], c_recv.at[d], (row, col, other)
        )

    order = (2, 6, 10, 14, 1, 3, 5, 7, 9, 11, 13, 15, 4, 8, 12)
    for d in order:
        c_copy(d).start()
    crecv[grp] = csend[grp]

    for copy in small:
        copy.wait()
    def column(ref, n):
        wide = jnp.broadcast_to(ref[...], (n, n))
        diagonal = lax.broadcasted_iota(jnp.int32, (n, n), 0) == lax.broadcasted_iota(
            jnp.int32, (n, n), 1
        )
        return jnp.sum(jnp.where(diagonal, wide, 0.0), axis=1, keepdims=True)

    occ = column(occ_ref, 128)
    orbital = lax.broadcasted_iota(jnp.int32, (128, 512), 0)
    first = jnp.sum(jnp.where(pair_ref[0:1, :] == orbital, occ, 0.0), axis=0, keepdims=True)
    second = jnp.sum(jnp.where(pair_ref[1:2, :] == orbital, occ, 0.0), axis=0, keepdims=True)
    energy = first + second
    pair = lax.broadcasted_iota(jnp.int32, (1, 512), 1)
    batch = column(batch_ref, 64)
    for i in range(2):
        for j in range(2):
            mine = (row * 2 + i) * 32 + grp * 2 + j
            one = jnp.sum(jnp.where(pair == mine, energy, 0.0), axis=1, keepdims=True)
            den[i, j] = one - batch - virt_ref[...]

    def block(step):
        from_zh = lax.rem(grp + step, 4)
        four_y = jnp.stack([crecv[i * 4 + from_zh] for i in range(4)])
        halves = four_y.astype(F32).reshape(4, 2, 8, 128)
        return [halves[:, j].reshape(32, 128).astype(BF16) for j in range(2)]

    def d_copy(dx, part):
        one = (dfar if part else dnear).at[x, core]
        sem = part * 3 + dx - 1
        return remote(one, one, d_send.at[sem], d_recv.at[sem], at(dx=dx))

    def e_copy(dx, part):
        one = (dfar if part else dnear).at[wrap(x - dx, NX), core]
        sem = part * 4 + dx
        return remote(one, one, e_send.at[sem], e_recv.at[sem], twin)

    for part in range(2):
        for d in reversed(order):
            if (d % 4 == 2) == (part == 1):
                c_copy(d).wait_recv()
        for place_here, step in enumerate((2,) if part else (0, 1, 3)):
            for j, half in enumerate(block(step)):
                to = dfar if part else dnear
                to[x, core, pl.ds(place_here * 32, 32), pl.ds(j * 128, 128)] = half
        for dx in (2, 1, 3):
            d_copy(dx, part).start()
        e_copy(0, part).start()
    for part in range(2):
        for dx in (1, 3, 2):
            d_copy(dx, part).wait_recv()
            e_copy(dx, part).start()

    def select(width, own_lane, zh_lane, core_lane):
        out_row = lax.broadcasted_iota(jnp.int32, (128, width), 0)
        lane = lax.broadcasted_iota(jnp.int32, (128, width), 1)
        same = (out_row % 64 // 16 == lane % 32 // 8) & (out_row % 2 == lane % 2)
        same = same & (core * 2 + out_row // 64 == lane % 8 // 2)
        same = same & (out_row % 16 // 4 == zh_lane(lane)) & own_lane(lane)
        same = same & (out_row % 4 // 2 == core_lane(lane))
        return jnp.where(same, 1.0, 0.0).astype(BF16)

    def near_zh(lane):
        return lax.rem(grp + jnp.where(lane // 32 == 2, 3, lane // 32), 4)

    picks = [
        select(128, lambda lane: lane < 96, near_zh, lambda lane: jnp.full_like(lane, c))
        for c in range(2)
    ]
    far_pick = select(
        256, lambda lane: lane // 64 == x, lambda lane: jnp.full_like(lane, lax.rem(grp + 2, 4)),
        lambda lane: lane // 32 % 2,
    )
    for dx in range(4):
        e_copy(dx, 0).wait_recv()
    total = jnp.zeros((128, 256), F32)
    for nx in range(4):
        for c in range(2):
            total = total + dot(kmat[nx * 2 + c, :, :96], dnear[nx, c])
    for c in range(2):
        total = total + dot(picks[c][:, :96], dnear[x, c])
    for dx in range(4):
        e_copy(dx, 1).wait_recv()
    far = dfar[...].reshape(256, 256)
    total = total + dot(kfar[...], far) + dot(far_pick, far)
    for i in range(2):
        for j in range(2):
            value = total[i * 64:(i + 1) * 64, j * 128:(j + 1) * 128] / den[i, j]
            out_ref[pl.ds(i * 128 + j, 64, stride=2), :] = value

    for t in range(-15, 17):
        if t:
            z_copy(t).wait_send()

    @pl.loop(0, ROUNDS)
    def _(q):
        y_plus(q).wait_send()
        y_minus(q).wait_send()

        @pl.when(q < DIRECT)
        def _():
            half_plus(q).wait_send()
            half_minus(q).wait_send()

        @pl.when(q >= DIRECT)
        def _():
            y_two(q).wait_send()

    for dx in range(4):
        s_copy(dx).wait_send()
        e_copy(dx, 0).wait_send()
        e_copy(dx, 1).wait_send()
        if dx:
            x_copy(dx).wait_send()
            d_copy(dx, 0).wait_send()
            d_copy(dx, 1).wait_send()
    for d in order:
        c_copy(d).wait_send()


def local(
    amplitudes, ladder_integrals, cycle_integrals, pair_list, occ_energy, batch_energy, virt_energy
):
    hbm = pl.BlockSpec(memory_space=pltpu.HBM)
    dma = pltpu.SemaphoreType.DMA
    counts = (7, 32, 32, 8, 8, 8, 8, 8, 8, 8, 8, 4, 4, 3, 3, 16, 16, 6, 6, 8, 8)
    out = pl.pallas_call(
        kernel,
        out_shape=pltpu.VMEM((256, 128), F32),
        in_specs=[hbm] * 7,
        out_specs=pl.BlockSpec(memory_space=pltpu.VMEM),
        scratch_shapes=[
            pltpu.VMEM((2, 512), jnp.int32),
            pltpu.VMEM((1, 128), F32),
            pltpu.VMEM((1, 64), F32),
            pltpu.VMEM((1, 128), F32),
            pltpu.VMEM((4, 32, 16, 512), BF16),
            pltpu.VMEM((8192, 128), BF16),
            pltpu.VMEM((1024, 128), F32),
            pltpu.VMEM((8, 256, 512), BF16),
            pltpu.VMEM((2, 4, 128, 256), F32),
            pltpu.VMEM((4, 128, 256), F32),
            pltpu.VMEM((2, 128, 256), F32),
            pltpu.VMEM((2, 128, 256), F32),
            pltpu.VMEM((2, 128, 256), BF16),
            pltpu.VMEM((256, 128), F32),
            pltpu.VMEM((16, 16, 128), BF16),
            pltpu.VMEM((16, 16, 128), BF16),
            pltpu.VMEM((4, 2, 96, 256), BF16),
            pltpu.VMEM((4, 2, 32, 256), BF16),
            pltpu.VMEM((2048, 64), BF16),
            pltpu.VMEM((2048, 64), F32),
            pltpu.VMEM((8, 128, 128), BF16),
            pltpu.VMEM((128, 256), BF16),
            pltpu.VMEM((2, 2, 64, 128), F32),
        ] + [dma((n,)) for n in counts],
        compiler_params=pltpu.CompilerParams(
            collective_id=0, has_side_effects=True, vmem_limit_bytes=60 * 1024 * 1024
        ),
    )(
        jnp.transpose(amplitudes, (1, 2, 0)).reshape(16, 512),
        ladder_integrals.reshape(8192, 128),
        cycle_integrals.reshape(16384, 64),
        jnp.transpose(pair_list),
        occ_energy.reshape(1, 128),
        batch_energy.reshape(1, 64),
        virt_energy.reshape(1, 128),
    )
    return out.reshape(2, 64, 2, 128)


def solution(mesh):
    placed = (
        P(None, "row", ("col", "grp")),
        P("row", None, "grp", "col"),
        P(),
        P(),
        P(),
        P(),
        P("col"),
    )
    return jax.shard_map(
        local, mesh=mesh, in_specs=placed, out_specs=P("row", None, "grp", "col"), check_vma=False
    )
```

```python
import jax
import jax.numpy as jnp
from jax import lax
from jax.experimental import pallas as pl
from jax.experimental.pallas import tpu as pltpu
from jax.sharding import PartitionSpec as P

MESH = pl.DeviceIdType.MESH
F32 = jnp.float32
BF16 = jnp.bfloat16
NX, NY, NZ = 4, 4, 32
ROUNDS = 8
DIRECT = 3


def dot(a, b, contract=((1,), (0,))):
    return lax.dot_general(a, b, (contract, ((), ())), preferred_element_type=F32)


def wrap(value, n):
    return lax.rem(value + 2 * n, n)


def kernel(
    amp_hbm, ladder_hbm, cycle_hbm, pair_hbm, occ_hbm, batch_hbm, virt_hbm, out_ref,
    pair_ref, occ_ref, batch_ref, virt_ref, buf, vraw, vwide, vmat, acc, sib, xsend, xrecv, ctmp, csend, crecv, dnear, dfar,
    kraw, kwide, kmat, kfar, den,
    in_sem, z_send, z_recv, yp_send, yp_recv, ym_send, ym_recv,
    hp_send, hp_recv, hm_send, hm_recv, s_send, s_recv, x_send, x_recv,
    c_send, c_recv, d_send, d_recv, e_send, e_recv,
):
    row = lax.axis_index("row")
    col = lax.axis_index("col")
    grp = lax.axis_index("grp")
    x, core = row // 2, lax.rem(row, 2)
    y = grp // 4
    z = lax.rem(grp, 4) * 8 + col

    def at(dx=0, dy=0, dz=0, flip=False):
        nx, ny, nz = wrap(x + dx, NX), wrap(y + dy, NY), wrap(z + dz, NZ)
        return (nx * 2 + (1 - core if flip else core), lax.rem(nz, 8), ny * 4 + nz // 8)

    def remote(src, dst, send, recv, device):
        return pltpu.make_async_remote_copy(
            src_ref=src, dst_ref=dst, send_sem=send, recv_sem=recv,
            device_id=device, device_id_type=MESH,
        )

    up, down = at(dy=1), at(dy=-1)
    twin = at(flip=True)

    own_copy = pltpu.make_async_copy(amp_hbm, buf.at[0, 0], in_sem.at[0])
    v_copy = pltpu.make_async_copy(ladder_hbm, vraw, in_sem.at[1])
    k_copy = pltpu.make_async_copy(
        cycle_hbm.at[pl.ds(pl.multiple_of(row * 2048, 2048), 2048), :], kraw, in_sem.at[2]
    )
    small = [
        pltpu.make_async_copy(src, dst, in_sem.at[3 + i])
        for i, (src, dst) in enumerate(
            ((pair_hbm, pair_ref), (occ_hbm, occ_ref), (batch_hbm, batch_ref), (virt_hbm, virt_ref))
        )
    ]
    barrier = pltpu.get_barrier_semaphore()
    near = [at(dz=d) for d in (4, -4, 3, -3, 2, -2, 1, -1)]
    near += [at(dy=2), up, down, at(dx=2), at(dx=1), at(dx=3), twin]
    for device in near:
        pl.semaphore_signal(barrier, inc=1, device_id=device, device_id_type=MESH)
    own_copy.start()
    v_copy.start()
    pl.semaphore_wait(barrier, len(near))

    def place(t):
        return 2 * t - 1 if t > 0 else -2 * t

    def z_copy(t):
        sign, far = (1, t) if t > 0 else (-1, -t)
        step = far % 4 or 4
        source = amp_hbm if far == step else buf.at[0, place(sign * (far - step))]
        return remote(
            source, buf.at[0, place(t)], z_send.at[place(t)], z_recv.at[place(t)], at(dz=sign * step)
        )

    def pass_on(*heads):
        for more in (4, 1, 2, 3):
            for sign, far in heads:
                if sign * (far + more) != -16:
                    z_copy(sign * (far + more)).start()

    def arrived(*shards):
        for t in shards:
            z_copy(t).wait_recv()

    def half_plus(q):
        return remote(
            buf.at[1, pl.ds(4 * q, 2)], buf.at[3, pl.ds(4 * q, 2)],
            hp_send.at[q], hp_recv.at[q], up,
        )

    def half_minus(q):
        return remote(
            buf.at[2, pl.ds(4 * q + 2, 2)], buf.at[3, pl.ds(4 * q + 2, 2)],
            hm_send.at[q], hm_recv.at[q], down,
        )

    def rows(q):
        return pl.ds(4 * q, 4) if q < 7 else pl.ds(2 * q + 14, 2)

    def y_two(q):
        return remote(buf.at[0, rows(q)], buf.at[3, rows(q)], hp_send.at[q], hp_recv.at[q], at(dy=2))

    def y_plus(q):
        return remote(buf.at[0, rows(q)], buf.at[1, rows(q)], yp_send.at[q], yp_recv.at[q], up)

    def y_minus(q):
        return remote(buf.at[0, rows(q)], buf.at[2, rows(q)], ym_send.at[q], ym_recv.at[q], down)

    pass_on((1, 0), (-1, 0))
    k_copy.start()
    for copy in small:
        copy.start()
    acc[...] = jnp.zeros_like(acc)
    own_copy.wait()
    v_copy.wait()

    def relayout(q):
        for slot, dy in enumerate((0, -1, 1, 2)):
            for e in range(4):
                dz = (2 * q, -2 * q - 1, 2 * q + 1, -2 * q - 2)[e]
                ny, nz = wrap(y + dy, NY), wrap(z + dz, NZ)
                shard = lax.rem(nz, 8) * 16 + ny * 4 + nz // 8
                for c in range(2):
                    start = pl.multiple_of(c * 4096 + shard * 32, 32)
                    to = ((slot * 4 + e) * 2 + c) * 32
                    vwide[pl.ds(to, 32), :] = vraw[pl.ds(start, 32), :].astype(F32)
        for a in range(4):
            vmat[q, :, pl.ds(a * 128, 128)] = vwide[pl.ds(a, 256, stride=4), :].astype(BF16)

    def multiply(q, block):
        lanes = pl.ds(pl.multiple_of(block * 128, 128), 128)
        lhs = buf[:, pl.ds(4 * q, 4), :, lanes].reshape(256, 128)
        product = dot(lhs, vmat[q], ((0,), (0,)))
        acc[0, block] += product[:, :256]
        acc[1, block] += product[:, 256:]

    @pl.loop(0, ROUNDS)
    def _(q):
        relayout(q)

    def y_start(q):
        if q >= DIRECT:
            y_two(q).start()
        y_plus(q).start()
        y_minus(q).start()

    def y_next(q):
        y_plus(q).wait_recv()
        if q < DIRECT:
            half_plus(q).start()
        y_minus(q).wait_recv()
        if q < DIRECT:
            half_minus(q).start()

    def y_done(q):
        if q >= DIRECT:
            y_two(q).wait_recv()
            return
        half_plus(q).wait_recv()
        half_minus(q).wait_recv()

    def products(q):
        y_done(q)

        @pl.loop(0, 4)
        def _(block):
            multiply(q, block)

    last = ROUNDS - 1
    arrived(1, -1, 2)
    y_start(0)
    arrived(-2, 3, -3, 4, -4)
    pass_on((1, 4), (-1, 4))
    y_start(1)
    y_next(0)
    arrived(5, -5, 6)
    y_start(2)
    y_next(1)
    arrived(-6, 7, -7, 8, -8)
    pass_on((1, 8), (-1, 8))
    y_start(3)
    products(0)
    y_next(2)
    products(1)
    arrived(9, -9, 10)
    y_start(4)
    y_next(3)
    arrived(-10, 11, -11, 12, -12)
    pass_on((1, 12), (-1, 12))
    y_start(5)
    products(2)
    products(3)
    y_next(4)
    arrived(13, -13, 14)
    y_start(6)
    y_next(5)
    arrived(-14, 15)
    y_start(7)
    arrived(-15, 16)
    y_start(8)
    products(4)
    products(5)
    y_next(6)
    products(6)
    for pair in (7, 8):
        y_next(pair)
        y_done(pair)

    def s_copy(dx):
        block = wrap(x + dx, NX)
        return remote(acc.at[1 - core, block], sib.at[block], s_send.at[dx], s_recv.at[dx], twin)

    def x_copy(dx):
        return remote(xsend.at[dx - 1], xrecv.at[dx - 1], x_send.at[dx - 1], x_recv.at[dx - 1], at(dx=dx))

    for dx in (2, 1, 3, 0):
        multiply(last, wrap(x + dx, NX))
        s_copy(dx).start()
    for dx in (2, 1, 3):
        block = wrap(x + dx, NX)
        s_copy(dx).wait_recv()
        xsend[dx - 1] = (acc[core, block] + sib[block]).astype(BF16)
        x_copy(dx).start()

    k_copy.wait()
    kwide[...] = kraw[...].astype(F32)
    from_c = lax.broadcasted_iota(jnp.int32, (64, 256), 0)
    lane = lax.broadcasted_iota(jnp.int32, (64, 256), 1)
    y_part = lane % 32 // 8 * 16 + lane % 2
    step_part = lane % 128 // 32
    from_zh = lax.rem(grp + jnp.where(step_part == 2, 3, step_part), 4)
    near_c = y_part + from_zh * 4 + lane // 128 * 2
    far_c = y_part + lax.rem(grp + 2, 4) * 4 + lane // 32 % 2 * 2
    far_total = jnp.zeros((128, 256), F32)
    for nx in range(4):
        total = jnp.zeros((128, 256), F32)
        for i in range(4):
            part = kwide[pl.ds(nx * 4 + i, 128, stride=16), :].astype(BF16)
            mine = lane % 8 // 2 == i
            total = total + dot(part, jnp.where(mine & (near_c == from_c), 1.0, 0.0).astype(BF16))
            mine = mine & (lane // 64 == nx) & (far_c == from_c)
            far_total = far_total + dot(part, jnp.where(mine, 1.0, 0.0).astype(BF16))
        kmat[nx * 2] = total[:, :128].astype(BF16)
        kmat[nx * 2 + 1] = total[:, 128:].astype(BF16)
    kfar[...] = far_total.astype(BF16)

    s_copy(0).wait_recv()
    ladder = acc[core, x] + sib[x]
    for dx in (1, 3, 2):
        x_copy(dx).wait_recv()
        ladder = ladder + xrecv[dx - 1].astype(F32)

    for i in range(4):
        for a in range(2):
            ctmp[pl.ds(i * 2 + a, 32, stride=8), :] = ladder[
                i * 32:(i + 1) * 32, a * 128:(a + 1) * 128
            ]
    csend[...] = ctmp[...].astype(BF16).reshape(16, 16, 128)

    def c_copy(d):
        other = lax.rem(grp + d, 16)
        return remote(
            csend.at[other], crecv.at[grp], c_send.at[d], c_recv.at[d], (row, col, other)
        )

    order = (2, 6, 10, 14, 1, 3, 5, 7, 9, 11, 13, 15, 4, 8, 12)
    for d in order:
        c_copy(d).start()
    crecv[grp] = csend[grp]

    for copy in small:
        copy.wait()
    def column(ref, n):
        wide = jnp.broadcast_to(ref[...], (n, n))
        diagonal = lax.broadcasted_iota(jnp.int32, (n, n), 0) == lax.broadcasted_iota(
            jnp.int32, (n, n), 1
        )
        return jnp.sum(jnp.where(diagonal, wide, 0.0), axis=1, keepdims=True)

    occ = column(occ_ref, 128)
    orbital = lax.broadcasted_iota(jnp.int32, (128, 512), 0)
    first = jnp.sum(jnp.where(pair_ref[0:1, :] == orbital, occ, 0.0), axis=0, keepdims=True)
    second = jnp.sum(jnp.where(pair_ref[1:2, :] == orbital, occ, 0.0), axis=0, keepdims=True)
    energy = first + second
    pair = lax.broadcasted_iota(jnp.int32, (1, 512), 1)
    batch = column(batch_ref, 64)
    for i in range(2):
        for j in range(2):
            mine = (row * 2 + i) * 32 + grp * 2 + j
            one = jnp.sum(jnp.where(pair == mine, energy, 0.0), axis=1, keepdims=True)
            den[i, j] = one - batch - virt_ref[...]

    for t in range(-15, 17):
        if t:
            z_copy(t).wait_send()

    for q in range(ROUNDS + 1):
        y_plus(q).wait_send()
        y_minus(q).wait_send()
        if q < DIRECT:
            half_plus(q).wait_send()
            half_minus(q).wait_send()
        else:
            y_two(q).wait_send()

    for dx in range(4):
        s_copy(dx).wait_send()
        if dx:
            x_copy(dx).wait_send()

    def block(step):
        from_zh = lax.rem(grp + step, 4)
        four_y = jnp.stack([crecv[i * 4 + from_zh] for i in range(4)])
        halves = four_y.astype(F32).reshape(4, 2, 8, 128)
        return [halves[:, j].reshape(32, 128).astype(BF16) for j in range(2)]

    def d_copy(dx, part):
        one = (dfar if part else dnear).at[x, core]
        sem = part * 3 + dx - 1
        return remote(one, one, d_send.at[sem], d_recv.at[sem], at(dx=dx))

    def e_copy(dx, part):
        one = (dfar if part else dnear).at[wrap(x - dx, NX), core]
        sem = part * 4 + dx
        return remote(one, one, e_send.at[sem], e_recv.at[sem], twin)

    for part in range(2):
        for d in reversed(order):
            if (d % 4 == 2) == (part == 1):
                c_copy(d).wait_recv()
        for place_here, step in enumerate((2,) if part else (0, 1, 3)):
            for j, half in enumerate(block(step)):
                to = dfar if part else dnear
                to[x, core, pl.ds(place_here * 32, 32), pl.ds(j * 128, 128)] = half
        for dx in (2, 1, 3):
            d_copy(dx, part).start()
        e_copy(0, part).start()
    for d in order:
        c_copy(d).wait_send()

    def select(width, own_lane, zh_lane, core_lane):
        out_row = lax.broadcasted_iota(jnp.int32, (128, width), 0)
        lane = lax.broadcasted_iota(jnp.int32, (128, width), 1)
        same = (out_row % 64 // 16 == lane % 32 // 8) & (out_row % 2 == lane % 2)
        same = same & (core * 2 + out_row // 64 == lane % 8 // 2)
        same = same & (out_row % 16 // 4 == zh_lane(lane)) & own_lane(lane)
        same = same & (out_row % 4 // 2 == core_lane(lane))
        return jnp.where(same, 1.0, 0.0).astype(BF16)

    def near_zh(lane):
        return lax.rem(grp + jnp.where(lane // 32 == 2, 3, lane // 32), 4)

    picks = [
        select(128, lambda lane: lane < 96, near_zh, lambda lane: jnp.full_like(lane, c))
        for c in range(2)
    ]
    far_pick = select(
        256, lambda lane: lane // 64 == x, lambda lane: jnp.full_like(lane, lax.rem(grp + 2, 4)),
        lambda lane: lane // 32 % 2,
    )
    for part in range(2):
        for dx in (1, 3, 2):
            d_copy(dx, part).wait_recv()
            e_copy(dx, part).start()

    for dx in range(4):
        e_copy(dx, 0).wait_recv()
    total = jnp.zeros((128, 256), F32)
    for nx in range(4):
        for c in range(2):
            total = total + dot(kmat[nx * 2 + c, :, :96], dnear[nx, c])
    for c in range(2):
        total = total + dot(picks[c][:, :96], dnear[x, c])
    for dx in range(4):
        e_copy(dx, 1).wait_recv()
    far = dfar[...].reshape(256, 256)
    total = total + dot(kfar[...], far) + dot(far_pick, far)
    for i in range(2):
        for j in range(2):
            value = total[i * 64:(i + 1) * 64, j * 128:(j + 1) * 128] / den[i, j]
            out_ref[pl.ds(i * 128 + j, 64, stride=2), :] = value

    for dx in range(4):
        for part in range(2):
            e_copy(dx, part).wait_send()
            if dx:
                d_copy(dx, part).wait_send()


def local(
    amplitudes, ladder_integrals, cycle_integrals, pair_list, occ_energy, batch_energy, virt_energy
):
    hbm = pl.BlockSpec(memory_space=pltpu.HBM)
    dma = pltpu.SemaphoreType.DMA
    counts = (7, 32, 32, 9, 9, 9, 9, 9, 9, 9, 9, 4, 4, 3, 3, 16, 16, 6, 6, 8, 8)
    out = pl.pallas_call(
        kernel,
        out_shape=pltpu.VMEM((256, 128), F32),
        in_specs=[hbm] * 7,
        out_specs=pl.BlockSpec(memory_space=pltpu.VMEM),
        scratch_shapes=[
            pltpu.VMEM((2, 512), jnp.int32),
            pltpu.VMEM((1, 128), F32),
            pltpu.VMEM((1, 64), F32),
            pltpu.VMEM((1, 128), F32),
            pltpu.VMEM((4, 32, 16, 512), BF16),
            pltpu.VMEM((8192, 128), BF16),
            pltpu.VMEM((1024, 128), F32),
            pltpu.VMEM((8, 256, 512), BF16),
            pltpu.VMEM((2, 4, 128, 256), F32),
            pltpu.VMEM((4, 128, 256), F32),
            pltpu.VMEM((3, 128, 256), BF16),
            pltpu.VMEM((3, 128, 256), BF16),
            pltpu.VMEM((256, 128), F32),
            pltpu.VMEM((16, 16, 128), BF16),
            pltpu.VMEM((16, 16, 128), BF16),
            pltpu.VMEM((4, 2, 96, 256), BF16),
            pltpu.VMEM((4, 2, 32, 256), BF16),
            pltpu.VMEM((2048, 64), BF16),
            pltpu.VMEM((2048, 64), F32),
            pltpu.VMEM((8, 128, 128), BF16),
            pltpu.VMEM((128, 256), BF16),
            pltpu.VMEM((2, 2, 64, 128), F32),
        ] + [dma((n,)) for n in counts],
        compiler_params=pltpu.CompilerParams(
            collective_id=0, has_side_effects=True, vmem_limit_bytes=60 * 1024 * 1024
        ),
    )(
        jnp.transpose(amplitudes, (1, 2, 0)).reshape(16, 512),
        ladder_integrals.reshape(8192, 128),
        cycle_integrals.reshape(16384, 64),
        jnp.transpose(pair_list),
        occ_energy.reshape(1, 128),
        batch_energy.reshape(1, 64),
        virt_energy.reshape(1, 128),
    )
    return out.reshape(2, 64, 2, 128)


def solution(mesh):
    placed = (
        P(None, "row", ("col", "grp")),
        P("row", None, "grp", "col"),
        P(),
        P(),
        P(),
        P(),
        P("col"),
    )
    return jax.shard_map(
        local, mesh=mesh, in_specs=placed, out_specs=P("row", None, "grp", "col"), check_vma=False
    )
```

```python
import jax
import jax.numpy as jnp
from jax import lax
from jax.experimental import pallas as pl
from jax.experimental.pallas import tpu as pltpu
from jax.sharding import PartitionSpec as P

MESH = pl.DeviceIdType.MESH
F32 = jnp.float32
BF16 = jnp.bfloat16
NX, NY, NZ = 4, 4, 32
ROUNDS = 8
DIRECT = 0


def dot(a, b, contract=((1,), (0,))):
    return lax.dot_general(a, b, (contract, ((), ())), preferred_element_type=F32)


def wrap(value, n):
    return lax.rem(value + 2 * n, n)


def kernel(
    amp_hbm, ladder_hbm, cycle_hbm, pair_hbm, occ_hbm, batch_hbm, virt_hbm, out_ref,
    pair_ref, occ_ref, batch_ref, virt_ref, buf, vraw, vwide, vmat, acc, sib, xsend, xrecv, ctmp, csend, crecv, dnear, dfar,
    kraw, kwide, kmat, kfar, den,
    in_sem, z_send, z_recv, yp_send, yp_recv, ym_send, ym_recv,
    hp_send, hp_recv, hm_send, hm_recv, s_send, s_recv, x_send, x_recv,
    c_send, c_recv, d_send, d_recv, e_send, e_recv,
):
    row = lax.axis_index("row")
    col = lax.axis_index("col")
    grp = lax.axis_index("grp")
    x, core = row // 2, lax.rem(row, 2)
    y = grp // 4
    z = lax.rem(grp, 4) * 8 + col

    def at(dx=0, dy=0, dz=0, flip=False):
        nx, ny, nz = wrap(x + dx, NX), wrap(y + dy, NY), wrap(z + dz, NZ)
        return (nx * 2 + (1 - core if flip else core), lax.rem(nz, 8), ny * 4 + nz // 8)

    def remote(src, dst, send, recv, device):
        return pltpu.make_async_remote_copy(
            src_ref=src, dst_ref=dst, send_sem=send, recv_sem=recv,
            device_id=device, device_id_type=MESH,
        )

    up, down = at(dy=1), at(dy=-1)
    twin = at(flip=True)

    own_copy = pltpu.make_async_copy(amp_hbm, buf.at[0, 0], in_sem.at[0])
    v_copy = pltpu.make_async_copy(ladder_hbm, vraw, in_sem.at[1])
    k_copy = pltpu.make_async_copy(
        cycle_hbm.at[pl.ds(pl.multiple_of(row * 2048, 2048), 2048), :], kraw, in_sem.at[2]
    )
    small = [
        pltpu.make_async_copy(src, dst, in_sem.at[3 + i])
        for i, (src, dst) in enumerate(
            ((pair_hbm, pair_ref), (occ_hbm, occ_ref), (batch_hbm, batch_ref), (virt_hbm, virt_ref))
        )
    ]
    barrier = pltpu.get_barrier_semaphore()
    near = [at(dz=d) for d in (4, -4, 3, -3, 2, -2, 1, -1)]
    near += [at(dy=2), up, down, at(dx=2), at(dx=1), at(dx=3), twin]
    for device in near:
        pl.semaphore_signal(barrier, inc=1, device_id=device, device_id_type=MESH)
    own_copy.start()
    v_copy.start()
    pl.semaphore_wait(barrier, len(near))

    def place(t):
        return 2 * t - 1 if t > 0 else -2 * t

    def z_copy(t):
        sign, far = (1, t) if t > 0 else (-1, -t)
        step = far % 4 or 4
        source = amp_hbm if far == step else buf.at[0, place(sign * (far - step))]
        return remote(
            source, buf.at[0, place(t)], z_send.at[place(t)], z_recv.at[place(t)], at(dz=sign * step)
        )

    def pass_on(*heads):
        for more in (4, 1, 2, 3):
            for sign, far in heads:
                if sign * (far + more) != -16:
                    z_copy(sign * (far + more)).start()

    def arrived(*shards):
        for t in shards:
            z_copy(t).wait_recv()

    def half_plus(q):
        return remote(
            buf.at[1, pl.ds(4 * q, 2)], buf.at[3, pl.ds(4 * q, 2)],
            hp_send.at[q], hp_recv.at[q], up,
        )

    def half_minus(q):
        return remote(
            buf.at[2, pl.ds(4 * q + 2, 2)], buf.at[3, pl.ds(4 * q + 2, 2)],
            hm_send.at[q], hm_recv.at[q], down,
        )

    def rows(q):
        return pl.ds(4 * q, 4) if q < 7 else pl.ds(2 * q + 14, 2)

    def y_two(q):
        return remote(buf.at[0, rows(q)], buf.at[3, rows(q)], hp_send.at[q], hp_recv.at[q], at(dy=2))

    def y_plus(q):
        return remote(buf.at[0, rows(q)], buf.at[1, rows(q)], yp_send.at[q], yp_recv.at[q], up)

    def y_minus(q):
        return remote(buf.at[0, rows(q)], buf.at[2, rows(q)], ym_send.at[q], ym_recv.at[q], down)

    pass_on((1, 0), (-1, 0))
    k_copy.start()
    for copy in small:
        copy.start()
    acc[...] = jnp.zeros_like(acc)
    own_copy.wait()
    v_copy.wait()

    def relayout(q):
        for slot, dy in enumerate((0, -1, 1, 2)):
            for e in range(4):
                dz = (2 * q, -2 * q - 1, 2 * q + 1, -2 * q - 2)[e]
                ny, nz = wrap(y + dy, NY), wrap(z + dz, NZ)
                shard = lax.rem(nz, 8) * 16 + ny * 4 + nz // 8
                for c in range(2):
                    start = pl.multiple_of(c * 4096 + shard * 32, 32)
                    to = ((slot * 4 + e) * 2 + c) * 32
                    vwide[pl.ds(to, 32), :] = vraw[pl.ds(start, 32), :].astype(F32)
        for a in range(4):
            vmat[q, :, pl.ds(a * 128, 128)] = vwide[pl.ds(a, 256, stride=4), :].astype(BF16)

    def multiply(q, block):
        lanes = pl.ds(pl.multiple_of(block * 128, 128), 128)
        lhs = buf[:, pl.ds(4 * q, 4), :, lanes].reshape(256, 128)
        product = dot(lhs, vmat[q], ((0,), (0,)))
        acc[0, block] += product[:, :256]
        acc[1, block] += product[:, 256:]

    @pl.loop(0, ROUNDS)
    def _(q):
        relayout(q)

    def y_start(q):
        if q >= DIRECT:
            y_two(q).start()
        y_plus(q).start()
        y_minus(q).start()

    def y_next(q):
        y_plus(q).wait_recv()
        if q < DIRECT:
            half_plus(q).start()
        y_minus(q).wait_recv()
        if q < DIRECT:
            half_minus(q).start()

    def y_done(q):
        if q >= DIRECT:
            y_two(q).wait_recv()
            return
        half_plus(q).wait_recv()
        half_minus(q).wait_recv()

    def products(q):
        y_done(q)

        @pl.loop(0, 4)
        def _(block):
            multiply(q, block)

    last = ROUNDS - 1
    arrived(1, -1, 2)
    y_start(0)
    arrived(-2, 3, -3, 4, -4)
    pass_on((1, 4), (-1, 4))
    y_start(1)
    y_next(0)
    arrived(5, -5, 6)
    y_start(2)
    arrived(-6, 7, -7, 8, -8)
    pass_on((1, 8), (-1, 8))
    y_start(3)
    y_next(1)
    products(0)
    arrived(9, -9, 10)
    y_start(4)
    arrived(-10, 11, -11, 12, -12)
    pass_on((1, 12), (-1, 12))
    y_start(5)
    y_next(2)
    products(1)
    arrived(13, -13, 14)
    y_start(6)
    arrived(-14, 15)
    y_start(7)
    arrived(-15, 16)
    y_start(8)
    products(2)
    for q in range(3, 7):
        y_next(q)
        products(q)
    for pair in (7, 8):
        y_next(pair)
        y_done(pair)

    def s_copy(dx):
        block = wrap(x + dx, NX)
        return remote(acc.at[1 - core, block], sib.at[block], s_send.at[dx], s_recv.at[dx], twin)

    def x_copy(dx):
        return remote(xsend.at[dx - 1], xrecv.at[dx - 1], x_send.at[dx - 1], x_recv.at[dx - 1], at(dx=dx))

    for dx in (2, 1, 3, 0):
        multiply(last, wrap(x + dx, NX))
        s_copy(dx).start()
    for dx in (2, 1, 3):
        block = wrap(x + dx, NX)
        s_copy(dx).wait_recv()
        xsend[dx - 1] = (acc[core, block] + sib[block]).astype(BF16)
        x_copy(dx).start()

    for t in range(-15, 17):
        if t:
            z_copy(t).wait_send()

    for q in range(ROUNDS + 1):
        y_plus(q).wait_send()
        y_minus(q).wait_send()
        if q < DIRECT:
            half_plus(q).wait_send()
            half_minus(q).wait_send()
        else:
            y_two(q).wait_send()

    s_copy(0).wait_recv()
    ladder = acc[core, x] + sib[x]
    for dx in (1, 3, 2):
        x_copy(dx).wait_recv()
        ladder = ladder + xrecv[dx - 1].astype(F32)

    for i in range(4):
        for a in range(2):
            ctmp[pl.ds(i * 2 + a, 32, stride=8), :] = ladder[
                i * 32:(i + 1) * 32, a * 128:(a + 1) * 128
            ]
    csend[...] = ctmp[...].astype(BF16).reshape(16, 16, 128)

    def c_copy(d):
        other = lax.rem(grp + d, 16)
        return remote(
            csend.at[other], crecv.at[grp], c_send.at[d], c_recv.at[d], (row, col, other)
        )

    order = (2, 6, 10, 14, 1, 3, 5, 7, 9, 11, 13, 15, 4, 8, 12)
    for d in order:
        c_copy(d).start()
    crecv[grp] = csend[grp]

    for copy in small:
        copy.wait()
    def column(ref, n):
        wide = jnp.broadcast_to(ref[...], (n, n))
        diagonal = lax.broadcasted_iota(jnp.int32, (n, n), 0) == lax.broadcasted_iota(
            jnp.int32, (n, n), 1
        )
        return jnp.sum(jnp.where(diagonal, wide, 0.0), axis=1, keepdims=True)

    occ = column(occ_ref, 128)
    orbital = lax.broadcasted_iota(jnp.int32, (128, 512), 0)
    first = jnp.sum(jnp.where(pair_ref[0:1, :] == orbital, occ, 0.0), axis=0, keepdims=True)
    second = jnp.sum(jnp.where(pair_ref[1:2, :] == orbital, occ, 0.0), axis=0, keepdims=True)
    energy = first + second
    pair = lax.broadcasted_iota(jnp.int32, (1, 512), 1)
    batch = column(batch_ref, 64)
    for i in range(2):
        for j in range(2):
            mine = (row * 2 + i) * 32 + grp * 2 + j
            one = jnp.sum(jnp.where(pair == mine, energy, 0.0), axis=1, keepdims=True)
            den[i, j] = one - batch - virt_ref[...]

    k_copy.wait()
    kwide[...] = kraw[...].astype(F32)
    from_c = lax.broadcasted_iota(jnp.int32, (64, 256), 0)
    lane = lax.broadcasted_iota(jnp.int32, (64, 256), 1)
    y_part = lane % 32 // 8 * 16 + lane % 2
    step_part = lane % 128 // 32
    from_zh = lax.rem(grp + jnp.where(step_part == 2, 3, step_part), 4)
    near_c = y_part + from_zh * 4 + lane // 128 * 2
    far_c = y_part + lax.rem(grp + 2, 4) * 4 + lane // 32 % 2 * 2
    far_total = jnp.zeros((128, 256), F32)
    for nx in range(4):
        total = jnp.zeros((128, 256), F32)
        for i in range(4):
            part = kwide[pl.ds(nx * 4 + i, 128, stride=16), :].astype(BF16)
            mine = lane % 8 // 2 == i
            total = total + dot(part, jnp.where(mine & (near_c == from_c), 1.0, 0.0).astype(BF16))
            mine = mine & (lane // 64 == nx) & (far_c == from_c)
            far_total = far_total + dot(part, jnp.where(mine, 1.0, 0.0).astype(BF16))
        kmat[nx * 2] = total[:, :128].astype(BF16)
        kmat[nx * 2 + 1] = total[:, 128:].astype(BF16)
    kfar[...] = far_total.astype(BF16)

    for dx in range(4):
        s_copy(dx).wait_send()
        if dx:
            x_copy(dx).wait_send()

    def block(step):
        from_zh = lax.rem(grp + step, 4)
        four_y = jnp.stack([crecv[i * 4 + from_zh] for i in range(4)])
        halves = four_y.astype(F32).reshape(4, 2, 8, 128)
        return [halves[:, j].reshape(32, 128).astype(BF16) for j in range(2)]

    def d_copy(dx, part):
        one = (dfar if part else dnear).at[x, core]
        sem = part * 3 + dx - 1
        return remote(one, one, d_send.at[sem], d_recv.at[sem], at(dx=dx))

    def e_copy(dx, part):
        one = (dfar if part else dnear).at[wrap(x - dx, NX), core]
        sem = part * 4 + dx
        return remote(one, one, e_send.at[sem], e_recv.at[sem], twin)

    for part in range(2):
        for d in reversed(order):
            if (d % 4 == 2) == (part == 1):
                c_copy(d).wait_recv()
        for place_here, step in enumerate((2,) if part else (0, 1, 3)):
            for j, half in enumerate(block(step)):
                to = dfar if part else dnear
                to[x, core, pl.ds(place_here * 32, 32), pl.ds(j * 128, 128)] = half
        for dx in (2, 1, 3):
            d_copy(dx, part).start()
        e_copy(0, part).start()
    for d in order:
        c_copy(d).wait_send()

    def select(width, own_lane, zh_lane, core_lane):
        out_row = lax.broadcasted_iota(jnp.int32, (128, width), 0)
        lane = lax.broadcasted_iota(jnp.int32, (128, width), 1)
        same = (out_row % 64 // 16 == lane % 32 // 8) & (out_row % 2 == lane % 2)
        same = same & (core * 2 + out_row // 64 == lane % 8 // 2)
        same = same & (out_row % 16 // 4 == zh_lane(lane)) & own_lane(lane)
        same = same & (out_row % 4 // 2 == core_lane(lane))
        return jnp.where(same, 1.0, 0.0).astype(BF16)

    def near_zh(lane):
        return lax.rem(grp + jnp.where(lane // 32 == 2, 3, lane // 32), 4)

    picks = [
        select(128, lambda lane: lane < 96, near_zh, lambda lane: jnp.full_like(lane, c))
        for c in range(2)
    ]
    far_pick = select(
        256, lambda lane: lane // 64 == x, lambda lane: jnp.full_like(lane, lax.rem(grp + 2, 4)),
        lambda lane: lane // 32 % 2,
    )
    for part in range(2):
        for dx in (1, 3, 2):
            d_copy(dx, part).wait_recv()
            e_copy(dx, part).start()

    for dx in range(4):
        e_copy(dx, 0).wait_recv()
    total = jnp.zeros((128, 256), F32)
    for nx in range(4):
        for c in range(2):
            total = total + dot(kmat[nx * 2 + c, :, :96], dnear[nx, c])
    for c in range(2):
        total = total + dot(picks[c][:, :96], dnear[x, c])
    for dx in range(4):
        e_copy(dx, 1).wait_recv()
    far = dfar[...].reshape(256, 256)
    total = total + dot(kfar[...], far) + dot(far_pick, far)
    for i in range(2):
        for j in range(2):
            value = total[i * 64:(i + 1) * 64, j * 128:(j + 1) * 128] / den[i, j]
            out_ref[pl.ds(i * 128 + j, 64, stride=2), :] = value

    for dx in range(4):
        for part in range(2):
            e_copy(dx, part).wait_send()
            if dx:
                d_copy(dx, part).wait_send()


def local(
    amplitudes, ladder_integrals, cycle_integrals, pair_list, occ_energy, batch_energy, virt_energy
):
    hbm = pl.BlockSpec(memory_space=pltpu.HBM)
    dma = pltpu.SemaphoreType.DMA
    counts = (7, 32, 32, 9, 9, 9, 9, 9, 9, 9, 9, 4, 4, 3, 3, 16, 16, 6, 6, 8, 8)
    out = pl.pallas_call(
        kernel,
        out_shape=pltpu.VMEM((256, 128), F32),
        in_specs=[hbm] * 7,
        out_specs=pl.BlockSpec(memory_space=pltpu.VMEM),
        scratch_shapes=[
            pltpu.VMEM((2, 512), jnp.int32),
            pltpu.VMEM((1, 128), F32),
            pltpu.VMEM((1, 64), F32),
            pltpu.VMEM((1, 128), F32),
            pltpu.VMEM((4, 32, 16, 512), BF16),
            pltpu.VMEM((8192, 128), BF16),
            pltpu.VMEM((1024, 128), F32),
            pltpu.VMEM((8, 256, 512), BF16),
            pltpu.VMEM((2, 4, 128, 256), F32),
            pltpu.VMEM((4, 128, 256), F32),
            pltpu.VMEM((3, 128, 256), BF16),
            pltpu.VMEM((3, 128, 256), BF16),
            pltpu.VMEM((256, 128), F32),
            pltpu.VMEM((16, 16, 128), BF16),
            pltpu.VMEM((16, 16, 128), BF16),
            pltpu.VMEM((4, 2, 96, 256), BF16),
            pltpu.VMEM((4, 2, 32, 256), BF16),
            pltpu.VMEM((2048, 64), BF16),
            pltpu.VMEM((2048, 64), F32),
            pltpu.VMEM((8, 128, 128), BF16),
            pltpu.VMEM((128, 256), BF16),
            pltpu.VMEM((2, 2, 64, 128), F32),
        ] + [dma((n,)) for n in counts],
        compiler_params=pltpu.CompilerParams(
            collective_id=0, has_side_effects=True, vmem_limit_bytes=60 * 1024 * 1024
        ),
    )(
        jnp.transpose(amplitudes, (1, 2, 0)).reshape(16, 512),
        ladder_integrals.reshape(8192, 128),
        cycle_integrals.reshape(16384, 64),
        jnp.transpose(pair_list),
        occ_energy.reshape(1, 128),
        batch_energy.reshape(1, 64),
        virt_energy.reshape(1, 128),
    )
    return out.reshape(2, 64, 2, 128)


def solution(mesh):
    placed = (
        P(None, "row", ("col", "grp")),
        P("row", None, "grp", "col"),
        P(),
        P(),
        P(),
        P(),
        P("col"),
    )
    return jax.shard_map(
        local, mesh=mesh, in_specs=placed, out_specs=P("row", None, "grp", "col"), check_vma=False
    )
```
